32 devices in a mesh: wide: 8 (over z, core), narrow: 4 (over y, x).
Axes of the slice: x: 2, y: 2, z: 4, core: 2. Of those that a mesh axis runs over, the one named last changes fastest.
Arguments:
- tokens: bfloat16 [2048, 1024], P('wide', 'narrow'), may hold values from -6 to 6
- gate_weight: bfloat16 [1024, 14784], P('wide', 'narrow'), may hold values from -0.1875 to 0.1875
- up_weight: bfloat16 [1024, 14784], P('wide', 'narrow'), may hold values from -0.1875 to 0.1875
Outputs:
- hidden: bfloat16 [2048, 14784], P('wide', 'narrow')
The draws below stay inside these ranges and needn't reach their ends.
All inputs are finite; a program needn't handle non-finite values.
Results may differ from the reference program's by a relative error of at most 0.001.
Values may be sent and summed in bfloat16 or wider, within the bound.
No kernel may reach another device: no remote copies, remote signals or barrier semaphores. Data moves between devices by JAX's collectives and lax.ppermute only.
A program may use at most 64 MiB of HBM per device.

```python
import math
import jax
import jax.numpy as jnp
from jax import lax

FF = 14784
K = 1024
TOKENS = 2048


def block_scale(own_key, extent, pieces, least, largest):
    level, own = 1.0, jax.random.fold_in(own_key, 6)
    for position, shards_of in pieces:
        draws = jnp.exp(jax.random.uniform(jax.random.fold_in(own, position), (shards_of,), jnp.float32, least / len(pieces), largest / len(pieces)))
        level = level * jnp.repeat(draws, extent[position] // shards_of).reshape([-1 if axis == position else 1 for axis in range(len(extent))])
    return level


def centred(stream_key, extent, deviation, most, pieces=(), dtype=jnp.bfloat16):
    result = jax.random.normal(stream_key, extent, jnp.float32) * deviation
    if len(pieces) > 0:
        result = block_scale(stream_key, extent, pieces, -0.22, 0.18) * result
    return jnp.clip(result, min=-most, max=most).astype(dtype)


def setup_inputs(seed: int = 0) -> dict:
    arg_keys = jax.random.split(jax.random.key(seed), 4)
    return {
        "tokens": centred(arg_keys[0], (TOKENS, K), 1.0, 6.0, ((0, 8), (1, 4))),
        "gate_weight": centred(arg_keys[1], (K, FF), K ** -0.5, 0.1875, ((0, 8), (1, 4))),
        "up_weight": centred(arg_keys[2], (K, FF), K ** -0.5, 0.1875, ((0, 8), (1, 4))),
    }


def reference(tokens, gate_weight, up_weight):
    block_rows = math.gcd(TOKENS, 1024)
    blocks = tokens.reshape(TOKENS // block_rows, block_rows, K)

    def project_block(rows):
        gate = jnp.dot(rows, gate_weight, preferred_element_type=jnp.float32)
        up = jnp.dot(rows, up_weight, preferred_element_type=jnp.float32)
        return (jax.nn.silu(gate) * up).astype(jnp.bfloat16)

    return lax.map(project_block, blocks).reshape(TOKENS, FF)
```

```python
import functools

import jax
import jax.numpy as jnp
from jax import lax
from jax.experimental import pallas as pl
from jax.experimental.pallas import tpu as pltpu
from jax.sharding import PartitionSpec as P

CORES = 2
LINE = 4
TILE = 16
SHARES = (46, 46)
TURN = (0, 3, 1, 2)
VMEM = 24 * 1024 * 1024
SMALL = 1024 * 1024
LARGE = 56 * 1024 * 1024


def gated(gate, up):
    return (jax.nn.silu(gate) * up).astype(jnp.bfloat16)


def gathered_everywhere(tokens, gate_weight, up_weight):
    rows = lax.all_gather(tokens, "narrow", axis=1, tiled=True)
    gate_full = lax.all_gather(gate_weight, "wide", axis=0, tiled=True)
    up_full = lax.all_gather(up_weight, "wide", axis=0, tiled=True)
    gate = jnp.dot(rows, gate_full, preferred_element_type=jnp.float32)
    up = jnp.dot(rows, up_full, preferred_element_type=jnp.float32)
    return gated(gate, up)


def line_position():
    index = lax.axis_index("wide")
    return index // CORES, index % CORES


def at_end():
    chip, _ = line_position()
    return (chip == 0) | (chip == LINE - 1)


def half_start(core, columns):
    return pl.multiple_of(core * (columns - half_of(columns)), TILE)


def half_of(columns):
    return -(-columns // (CORES * TILE)) * TILE


def copy_all(copies):
    for copy in copies:
        copy.start()
    for copy in copies:
        copy.wait()


def cut_kernel(gate_ref, up_ref, out_ref, sems):
    _, core = line_position()
    columns = gate_ref.shape[0]
    half = half_of(columns)
    theirs = pl.ds(half_start(1 - core, columns), half)
    copy_all(
        [
            pltpu.make_async_copy(w.at[theirs], out_ref.at[pl.ds(k * half, half)], sems.at[k])
            for k, w in enumerate((gate_ref, up_ref))
        ]
    )


def cut(gate_t, up_t):
    columns, depth = gate_t.shape
    in_hbm = pl.BlockSpec(memory_space=pltpu.HBM)
    return pl.pallas_call(
        cut_kernel,
        in_specs=[in_hbm, in_hbm],
        out_specs=pl.BlockSpec(memory_space=pltpu.VMEM),
        out_shape=jax.ShapeDtypeStruct((2 * half_of(columns), depth), gate_t.dtype),
        scratch_shapes=[pltpu.SemaphoreType.DMA((2,))],
        compiler_params=pltpu.CompilerParams(vmem_limit_bytes=LARGE),
        cost_estimate=pl.CostEstimate(flops=0, bytes_accessed=4 * gate_t.size, transcendentals=0),
        name="cut",
    )(gate_t, up_t)


def pack_kernel(chunks, places, gate_ref, up_ref, got_ref, *refs):
    outs, sems = refs[:-1], refs[-1]
    _, core = line_position()
    columns, depth = gate_ref.shape
    half = half_of(columns)
    first = half_start(core, columns)

    def fill(me):
        copies = []
        for o, row, i in places:
            start, size = chunks[i]
            for k, w in enumerate((gate_ref, up_ref)):
                target = outs[o].at[pl.ds(row + k * size, size)]
                mine = target.at[:, pl.ds(me * depth, depth)]
                other = target.at[:, pl.ds((1 - me) * depth, depth)]
                sources = (w.at[pl.ds(first + start, size)], mine), (got_ref.at[pl.ds(k * half + start, size)], other)
                for source, target_part in sources:
                    copies.append(pltpu.make_async_copy(source, target_part, sems.at[len(copies)]))
        copy_all(copies)

    for me in range(CORES):
        pl.when(core == me)(functools.partial(fill, me))


def pack(gate_t, up_t, got, chunks, wanted):
    depth = gate_t.shape[1]
    in_hbm = pl.BlockSpec(memory_space=pltpu.HBM)
    whole = pl.BlockSpec(memory_space=pltpu.VMEM)
    places, out_shape = [], []
    for o, group in enumerate(wanted):
        row = 0
        for i in group:
            places.append((o, row, i))
            row += 2 * chunks[i][1]
        out_shape.append(jax.ShapeDtypeStruct((row, CORES * depth), gate_t.dtype))
    return pl.pallas_call(
        functools.partial(pack_kernel, chunks, places),
        in_specs=[in_hbm, in_hbm, whole],
        out_specs=[whole] * len(wanted),
        out_shape=out_shape,
        scratch_shapes=[pltpu.SemaphoreType.DMA((4 * len(places),))],
        compiler_params=pltpu.CompilerParams(vmem_limit_bytes=SMALL),
        cost_estimate=pl.CostEstimate(flops=0, bytes_accessed=8 * gate_t.size, transcendentals=0),
        name="pack",
    )(gate_t, up_t, got)


def turn_kernel(own_ref, outer_ref, out_ref):
    rows = own_ref.shape[0]
    out_ref[:, :rows] = own_ref[...].T
    out_ref[:, rows:] = outer_ref[...].T


def turn(own, outer):
    rows, features = own.shape
    return pl.pallas_call(
        turn_kernel,
        in_specs=[pl.BlockSpec(memory_space=pltpu.VMEM)] * 2,
        out_specs=pl.BlockSpec(memory_space=pltpu.VMEM),
        out_shape=jax.ShapeDtypeStruct((features, 2 * rows), own.dtype),
        compiler_params=pltpu.CompilerParams(vmem_limit_bytes=4 * SMALL),
        cost_estimate=pl.CostEstimate(flops=0, bytes_accessed=8 * own.size, transcendentals=0),
        name="turn",
    )(own, outer)


def arrange_kernel(*refs):
    blocks, out_ref, sems = refs[:LINE], refs[LINE], refs[LINE + 1]
    chip, _ = line_position()
    group = lax.axis_index("narrow")
    features = blocks[0].shape[0]
    copies = []
    for d, block in enumerate(blocks):
        want = chip ^ group ^ d
        place = jnp.where(want == TURN[1], 1, jnp.where(want == TURN[2], 2, jnp.where(want == TURN[3], 3, 0)))
        row = pl.multiple_of(place * features, features)
        copies.append(pltpu.make_async_copy(block, out_ref.at[pl.ds(row, features)], sems.at[d]))
    copy_all(copies)


def arrange(blocks):
    features, rows = blocks[0].shape
    whole = pl.BlockSpec(memory_space=pltpu.VMEM)
    return pl.pallas_call(
        arrange_kernel,
        in_specs=[whole] * LINE,
        out_specs=whole,
        out_shape=jax.ShapeDtypeStruct((LINE * features, rows), blocks[0].dtype),
        scratch_shapes=[pltpu.SemaphoreType.DMA((LINE,))],
        compiler_params=pltpu.CompilerParams(vmem_limit_bytes=SMALL),
        cost_estimate=pl.CostEstimate(flops=0, bytes_accessed=4 * LINE * blocks[0].size, transcendentals=0),
        name="arrange",
    )(*blocks)


def store(result_ref, parts, sems, at=0):
    _, core = line_position()
    columns = result_ref.shape[0]
    copies = []
    for k, (ref, others, start) in enumerate(parts):
        first = half_start(1 - core if others else core, columns) + start
        target = result_ref.at[pl.ds(first, ref.shape[0])]
        copies.append(pltpu.make_async_copy(ref, target, sems.at[at + k]))
    return copies


def chunk_kernel(plan, x_ref, y_ref, *refs):
    start, step, joint, swap_stores, back_start, weight_rows = plan
    weights, refs = refs[:LINE], refs[LINE:]
    own_buf, sems = refs[-2:]
    size, rows = own_buf.shape
    result_ref, swap_ref, *outers = refs[-5 if joint else -6 : -2]
    if joint:
        outers = outers[0].at[:, pl.ds(0, rows)], outers[0].at[:, pl.ds(rows, rows)]

    def swap_store(k):
        if swap_stores is None or swap_stores[k] is None:
            return []
        first, count = swap_stores[k]
        return store(result_ref, [(refs[0].at[pl.ds(0, count)], True, first)], sems, 1)

    @pl.when(jnp.logical_not(at_end()))
    def _():
        copies = swap_store(0)
        for copy in copies:
            copy.start()
        for j in range(0, size, step):
            sides = [
                jnp.concatenate([w[pl.ds(r + k * size + j, step), :] for w, r in zip(weights, weight_rows)], axis=1)
                for k in (0, 1)
            ]
            both_w = jnp.concatenate(sides, axis=0)
            here = pl.ds(j, step)
            for tokens_ref, own_out, outer_out in ((x_ref, own_buf, outers[0]), (y_ref, swap_ref, outers[1])):
                both = jnp.dot(both_w, tokens_ref[...], preferred_element_type=jnp.float32)
                hidden = gated(both[:step], both[step:])
                own_out[here, :] = hidden[:, :rows]
                outer_out[here, :] = hidden[:, rows:]
        copies += store(result_ref, [(own_buf, False, start)], sems)
        copies[-1].start()
        for copy in copies:
            copy.wait()

    if back_start is not None:
        back_ref = refs[1]

        @pl.when(at_end())
        def _():
            count = back_ref.shape[0]
            mine = back_ref.at[:, pl.ds(0, rows)]
            copies = store(result_ref, [(mine, False, back_start)], sems) + swap_store(1)
            copies.append(
                pltpu.make_async_copy(back_ref.at[:, pl.ds(rows, rows)], swap_ref.at[pl.ds(0, count)], sems.at[2])
            )
            copy_all(copies)


def chunk_hidden(x, y, weights, start, size, step, result, joint, swapped=None, back=None):
    rows = x.shape[1] // 2
    whole = pl.BlockSpec(memory_space=pltpu.VMEM)
    in_hbm = pl.BlockSpec(memory_space=pltpu.HBM)
    operands = [x, y] + [w for w, _ in weights]
    swap_rows = size
    if swapped is not None:
        operands.append(swapped[0])
    if back is not None:
        operands.append(back[0])
        swap_rows = max(size, back[0].shape[0])
    in_specs = [whole] * len(operands)
    aliases = {}
    if not isinstance(result, jax.ShapeDtypeStruct):
        aliases = {len(operands): 0}
        operands.append(result)
        in_specs.append(in_hbm)
    out_shape = [jax.ShapeDtypeStruct(result.shape, result.dtype), jax.ShapeDtypeStruct((swap_rows, rows), result.dtype)]
    out_shape += [jax.ShapeDtypeStruct((size, rows * (2 if joint else 1)), result.dtype)] * (1 if joint else 2)
    plan = (start, step, joint, swapped and swapped[1], back and back[1], [r for _, r in weights])
    return pl.pallas_call(
        functools.partial(chunk_kernel, plan),
        in_specs=in_specs,
        out_specs=[in_hbm] + [whole] * (len(out_shape) - 1),
        out_shape=out_shape,
        scratch_shapes=[pltpu.VMEM((size, rows), result.dtype), pltpu.SemaphoreType.DMA((3,))],
        input_output_aliases=aliases,
        compiler_params=pltpu.CompilerParams(vmem_limit_bytes=VMEM),
        cost_estimate=pl.CostEstimate(flops=0, bytes_accessed=2 * size * rows, transcendentals=0),
        name="chunk_hidden",
    )(*operands)


def put_kernel(stores, *refs):
    result_ref, sems = refs[-2:]
    for end in (0, 1):

        @pl.when(at_end() == (end == 1))
        def _():
            parts = [
                (refs[k].at[pl.ds(0, count)], others, first) for k, others, first, count in stores[end]
            ]
            copy_all(store(result_ref, parts, sems))


def put(result, arrays, stores):
    in_hbm = pl.BlockSpec(memory_space=pltpu.HBM)
    return pl.pallas_call(
        functools.partial(put_kernel, stores),
        in_specs=[pl.BlockSpec(memory_space=pltpu.VMEM)] * len(arrays) + [in_hbm],
        out_specs=in_hbm,
        out_shape=jax.ShapeDtypeStruct(result.shape, result.dtype),
        scratch_shapes=[pltpu.SemaphoreType.DMA((len(arrays),))],
        input_output_aliases={len(arrays): 0},
        compiler_params=pltpu.CompilerParams(vmem_limit_bytes=SMALL),
        cost_estimate=pl.CostEstimate(flops=0, bytes_accessed=4 * arrays[0].size, transcendentals=0),
        name="put",
    )(*arrays, result)


def after(x, *earlier):
    return lax.optimization_barrier((x, *earlier))[0]


def folded(tokens, gate_weight, up_weight):
    rows_own = tokens.shape[0]
    columns_dev = gate_weight.shape[1]

    def between(pairs, cross=0):
        return [(s * CORES + c, t * CORES + (c ^ cross)) for s, t in pairs for c in range(CORES)]

    inward = between([(0, 1), (3, 2)])
    outward = between([(1, 0), (2, 3)])
    outward_cross = between([(1, 0), (2, 3)], 1)
    across = between([(1, 2), (2, 1)])
    other_core = [(i, i ^ 1) for i in range(LINE * CORES)]

    def send(x, pairs):
        return lax.ppermute(x, "wide", pairs)

    tiles = half_of(columns_dev) // TILE
    counts = [tiles * p // 116 for p in SHARES]
    counts.append(tiles - sum(counts))
    h = [TILE * t for t in counts]
    starts = [sum(h[:i]) for i in range(3)]

    mine = gate_weight.T, up_weight.T
    outer_tokens = send(tokens, inward)
    got = after(send(cut(*mine), other_core), outer_tokens)
    chunks = list(zip(starts, h))
    pack_01, pack_0 = pack(*mine, got, chunks, ((0, 1), (0,)))
    pack_1, pack_2 = pack(*mine, got, chunks, ((1,), (2,)))

    own_01 = send(pack_01, across)
    outer_0 = send(pack_0, inward)
    outer_1 = send(pack_1, inward)
    outer_2 = send(after(pack_2, outer_0), inward)
    far_0 = send(outer_0, across)

    both = turn(after(tokens, pack_0), outer_tokens)
    blocks = [both] + [lax.ppermute(both, "narrow", [(i, i ^ d) for i in range(LINE)]) for d in (1, 2, 3)]
    x = arrange(blocks)
    y = send(x, other_core)

    far_1 = send(after(outer_1, own_01), across)
    own_2 = send(after(pack_2, far_0), across)
    far_2 = send(after(outer_2, far_1), across)
    second = 2 * h[0]
    weights = [
        [(pack_01, 0), (own_01, 0), (outer_0, 0), (far_0, 0)],
        [(pack_01, second), (own_01, second), (outer_1, 0), (far_1, 0)],
        [(pack_2, 0), (own_2, 0), (outer_2, 0), (far_2, 0)],
    ]

    def compute(i, result, joint, **options):
        step = h[i] if h[i] <= 384 else h[i] // 2
        return chunk_hidden(x, y, weights[i], starts[i], h[i], step, result, joint, **options)

    result = jax.ShapeDtypeStruct((columns_dev, rows_own), jnp.bfloat16)
    result, swap, out = compute(0, result, True)
    back_0 = send(out, outward)
    swapped_0 = send(swap, other_core)
    result, swap, same, cross = compute(1, result, False, swapped=(swapped_0, (chunks[0], None)))
    back_1 = send(same, outward), send(cross, outward_cross)
    swapped_1 = send(swap, other_core)
    result, swap, same, cross = compute(
        2, result, False, swapped=(swapped_1, (chunks[1], None)), back=(back_0, starts[0])
    )
    back_2 = send(same, outward), send(cross, outward_cross)
    swapped_2 = send(swap, other_core)
    stores = [(0, True, *chunks[2])], [(0, True, *chunks[0]), (1, False, *chunks[1]), (2, True, *chunks[1])]
    result = put(result, (swapped_2, *back_1), stores)
    return put(result, back_2, ([], [(0, False, *chunks[2]), (1, True, *chunks[2])])).T


def solution(mesh):
    in_specs = (P("wide", "narrow"), P("wide", "narrow"), P("wide", "narrow"))
    out_specs = P("wide", "narrow")
    local = folded if mesh.shape["wide"] == LINE * CORES else gathered_everywhere
    return jax.shard_map(local, mesh=mesh, in_specs=in_specs, out_specs=out_specs, check_vma=False)
```

```python
import functools

import jax
import jax.numpy as jnp
from jax import lax
from jax.experimental import pallas as pl
from jax.experimental.pallas import tpu as pltpu
from jax.sharding import PartitionSpec as P

CORES = 2
LINE = 4
TILE = 16
SHARES = (44, 46)
TURN = (0, 3, 1, 2)
VMEM = 24 * 1024 * 1024
SMALL = 1024 * 1024
LARGE = 56 * 1024 * 1024


def gated(gate, up):
    return (jax.nn.silu(gate) * up).astype(jnp.bfloat16)


def gathered_everywhere(tokens, gate_weight, up_weight):
    rows = lax.all_gather(tokens, "narrow", axis=1, tiled=True)
    gate_full = lax.all_gather(gate_weight, "wide", axis=0, tiled=True)
    up_full = lax.all_gather(up_weight, "wide", axis=0, tiled=True)
    gate = jnp.dot(rows, gate_full, preferred_element_type=jnp.float32)
    up = jnp.dot(rows, up_full, preferred_element_type=jnp.float32)
    return gated(gate, up)


def line_position():
    index = lax.axis_index("wide")
    return index // CORES, index % CORES


def at_end():
    chip, _ = line_position()
    return (chip == 0) | (chip == LINE - 1)


def half_start(core, columns):
    return pl.multiple_of(core * (columns - half_of(columns)), TILE)


def half_of(columns):
    return -(-columns // (CORES * TILE)) * TILE


def copy_all(copies):
    for copy in copies:
        copy.start()
    for copy in copies:
        copy.wait()


def strips(size):
    strip = -(-size // (4 * TILE)) * TILE
    return [(at, min(strip, size - at)) for at in range(0, size, strip)]


def cut_kernel(start, size, gate_ref, up_ref, out_ref, sems):
    _, core = line_position()
    theirs = half_start(1 - core, gate_ref.shape[0]) + start
    copies = []
    for k, w in enumerate((gate_ref, up_ref)):
        for at, count in strips(size):
            target = out_ref.at[pl.ds(k * size + at, count)]
            copies.append(pltpu.make_async_copy(w.at[pl.ds(theirs + at, count)], target, sems.at[len(copies)]))
    copy_all(copies)


def cut(gate_t, up_t, start, size, room):
    in_hbm = pl.BlockSpec(memory_space=pltpu.HBM)
    return pl.pallas_call(
        functools.partial(cut_kernel, start, size),
        in_specs=[in_hbm, in_hbm],
        out_specs=pl.BlockSpec(memory_space=pltpu.VMEM),
        out_shape=jax.ShapeDtypeStruct((2 * size, gate_t.shape[1]), gate_t.dtype),
        scratch_shapes=[pltpu.SemaphoreType.DMA((8,))],
        compiler_params=pltpu.CompilerParams(vmem_limit_bytes=room),
        cost_estimate=pl.CostEstimate(flops=0, bytes_accessed=4 * gate_t.size, transcendentals=0),
        name="cut",
    )(gate_t, up_t)


def pack_kernel(chunks, got_start, places, gate_ref, up_ref, got_ref, *refs):
    outs, sems = refs[:-1], refs[-1]
    _, core = line_position()
    columns, depth = gate_ref.shape
    got_size = got_ref.shape[0] // 2
    first = half_start(core, columns)

    def fill(me):
        copies = []
        for o, row, i in places:
            start, size = chunks[i]
            for k, w in enumerate((gate_ref, up_ref)):
                target = outs[o].at[pl.ds(row + k * size, size)]
                mine = target.at[:, pl.ds(me * depth, depth)]
                other = target.at[:, pl.ds((1 - me) * depth, depth)]
                sources = (w.at[pl.ds(first + start, size)], mine), (
                    got_ref.at[pl.ds(k * got_size + start - got_start, size)],
                    other,
                )
                for source, target_part in sources:
                    copies.append(pltpu.make_async_copy(source, target_part, sems.at[len(copies)]))
        copy_all(copies)

    for me in range(CORES):
        pl.when(core == me)(functools.partial(fill, me))


def pack(gate_t, up_t, got, got_start, chunks, wanted):
    depth = gate_t.shape[1]
    in_hbm = pl.BlockSpec(memory_space=pltpu.HBM)
    whole = pl.BlockSpec(memory_space=pltpu.VMEM)
    places, out_shape = [], []
    for o, group in enumerate(wanted):
        row = 0
        for i in group:
            places.append((o, row, i))
            row += 2 * chunks[i][1]
        out_shape.append(jax.ShapeDtypeStruct((row, CORES * depth), gate_t.dtype))
    return pl.pallas_call(
        functools.partial(pack_kernel, chunks, got_start, places),
        in_specs=[in_hbm, in_hbm, whole],
        out_specs=[whole] * len(wanted),
        out_shape=out_shape,
        scratch_shapes=[pltpu.SemaphoreType.DMA((4 * len(places),))],
        compiler_params=pltpu.CompilerParams(vmem_limit_bytes=SMALL),
        cost_estimate=pl.CostEstimate(flops=0, bytes_accessed=8 * gate_t.size, transcendentals=0),
        name="pack",
    )(gate_t, up_t, got)


def arrange_kernel(*refs):
    blocks, outs = refs[:LINE], refs[LINE:]
    chip, _ = line_position()
    group = lax.axis_index("narrow")
    features = blocks[0].shape[1]
    for d, block in enumerate(blocks):
        turned = block[...].T
        for out, at in zip(outs, (chip, chip ^ 1)):
            want = at ^ group ^ d
            place = jnp.where(want == TURN[1], 1, jnp.where(want == TURN[2], 2, jnp.where(want == TURN[3], 3, 0)))
            out[pl.ds(pl.multiple_of(place * features, features), features), :] = turned


def arrange(blocks):
    rows, features = blocks[0].shape
    whole = pl.BlockSpec(memory_space=pltpu.VMEM)
    return pl.pallas_call(
        arrange_kernel,
        in_specs=[whole] * LINE,
        out_specs=[whole] * 2,
        out_shape=[jax.ShapeDtypeStruct((LINE * features, rows), blocks[0].dtype)] * 2,
        compiler_params=pltpu.CompilerParams(vmem_limit_bytes=4 * SMALL),
        cost_estimate=pl.CostEstimate(flops=0, bytes_accessed=4 * LINE * blocks[0].size, transcendentals=0),
        name="arrange",
    )(*blocks)


def store(result_ref, parts, sems, at=0):
    _, core = line_position()
    columns = result_ref.shape[0]
    copies = []
    for k, (ref, others, start) in enumerate(parts):
        first = half_start(1 - core if others else core, columns) + start
        target = result_ref.at[pl.ds(first, ref.shape[0])]
        copies.append(pltpu.make_async_copy(ref, target, sems.at[at + k]))
    return copies


def products(blocks, weights, tokens, outs):
    for j, step, sources in blocks:
        sides = [
            jnp.concatenate([weights[source[0]][pl.ds(source[k], step), :] for source in sources], axis=1)
            for k in (1, 2)
        ]
        both_w = jnp.concatenate(sides, axis=0)
        for tokens_ref, out in zip(tokens, outs):
            both = jnp.dot(both_w, tokens_ref[...], preferred_element_type=jnp.float32)
            out[pl.ds(j, step), :] = gated(both[:step], both[step:])


def outer_kernel(blocks, count, *refs):
    tokens, weights, outs = refs[:2], refs[2 : 2 + count], refs[2 + count :]
    rows = tokens[0].shape[1]
    if len(outs) == 1:
        outs = outs[0].at[:, pl.ds(0, rows)], outs[0].at[:, pl.ds(rows, rows)]
    pl.when(jnp.logical_not(at_end()))(functools.partial(products, blocks, weights, tokens, outs))


def outer_hidden(tokens, weights, blocks, size, joint):
    features, rows = tokens[0].shape
    whole = pl.BlockSpec(memory_space=pltpu.VMEM)
    return pl.pallas_call(
        functools.partial(outer_kernel, blocks, len(weights)),
        in_specs=[whole] * (2 + len(weights)),
        out_specs=[whole] * (1 if joint else 2),
        out_shape=[jax.ShapeDtypeStruct((size, rows * (2 if joint else 1)), tokens[0].dtype)] * (1 if joint else 2),
        compiler_params=pltpu.CompilerParams(vmem_limit_bytes=VMEM),
        cost_estimate=pl.CostEstimate(flops=0, bytes_accessed=2 * size * rows, transcendentals=0),
        name="outer_hidden",
    )(*tokens, *weights)


def own_kernel(plan, *refs):
    start, blocks, swap_stores, back_start, count = plan
    tokens, weights, refs = refs[:2], refs[2 : 2 + count], refs[2 + count :]
    result_ref, swap_ref, own_buf, sems = refs[-4:]
    rows = own_buf.shape[1]

    def swap_store(k):
        if swap_stores is None or swap_stores[k] is None:
            return []
        first, number = swap_stores[k]
        return store(result_ref, [(refs[0].at[pl.ds(0, number)], True, first)], sems, 1)

    @pl.when(jnp.logical_not(at_end()))
    def _():
        copies = swap_store(0)
        for copy in copies:
            copy.start()
        products(blocks, weights, tokens, (own_buf, swap_ref))
        copies += store(result_ref, [(own_buf, False, start)], sems)
        copies[-1].start()
        for copy in copies:
            copy.wait()

    @pl.when(at_end())
    def _():
        copies = swap_store(1)
        if back_start is not None:
            back_ref = refs[1]
            number = back_ref.shape[0]
            copies += store(result_ref, [(back_ref.at[:, pl.ds(0, rows)], False, back_start)], sems)
            copies.append(
                pltpu.make_async_copy(back_ref.at[:, pl.ds(rows, rows)], swap_ref.at[pl.ds(0, number)], sems.at[2])
            )
        copy_all(copies)


def own_hidden(tokens, weights, blocks, start, size, result, swapped=None, back=None):
    rows = tokens[0].shape[1]
    whole = pl.BlockSpec(memory_space=pltpu.VMEM)
    in_hbm = pl.BlockSpec(memory_space=pltpu.HBM)
    operands = [*tokens, *weights]
    swap_rows = size
    if swapped is not None:
        operands.append(swapped[0])
    if back is not None:
        operands.append(back[0])
        swap_rows = max(size, back[0].shape[0])
    in_specs = [whole] * len(operands)
    aliases = {}
    if not isinstance(result, jax.ShapeDtypeStruct):
        aliases = {len(operands): 0}
        operands.append(result)
        in_specs.append(in_hbm)
    plan = (start, blocks, swapped and swapped[1], back and back[1], len(weights))
    return pl.pallas_call(
        functools.partial(own_kernel, plan),
        in_specs=in_specs,
        out_specs=[in_hbm, whole],
        out_shape=[
            jax.ShapeDtypeStruct(result.shape, result.dtype),
            jax.ShapeDtypeStruct((swap_rows, rows), result.dtype),
        ],
        scratch_shapes=[pltpu.VMEM((size, rows), result.dtype), pltpu.SemaphoreType.DMA((3,))],
        input_output_aliases=aliases,
        compiler_params=pltpu.CompilerParams(vmem_limit_bytes=VMEM),
        cost_estimate=pl.CostEstimate(flops=0, bytes_accessed=2 * size * rows, transcendentals=0),
        name="own_hidden",
    )(*operands)


def put_kernel(stores, *refs):
    result_ref, sems = refs[-2:]
    for end in (0, 1):

        @pl.when(at_end() == (end == 1))
        def _():
            parts = [
                (refs[k].at[pl.ds(0, count)], others, first) for k, others, first, count in stores[end]
            ]
            copy_all(store(result_ref, parts, sems))


def put(result, arrays, stores):
    in_hbm = pl.BlockSpec(memory_space=pltpu.HBM)
    return pl.pallas_call(
        functools.partial(put_kernel, stores),
        in_specs=[pl.BlockSpec(memory_space=pltpu.VMEM)] * len(arrays) + [in_hbm],
        out_specs=in_hbm,
        out_shape=jax.ShapeDtypeStruct(result.shape, result.dtype),
        scratch_shapes=[pltpu.SemaphoreType.DMA((len(arrays),))],
        input_output_aliases={len(arrays): 0},
        compiler_params=pltpu.CompilerParams(vmem_limit_bytes=SMALL),
        cost_estimate=pl.CostEstimate(flops=0, bytes_accessed=4 * arrays[0].size, transcendentals=0),
        name="put",
    )(*arrays, result)


def after(x, *earlier):
    return lax.optimization_barrier((x, *earlier))[0]


def folded(tokens, gate_weight, up_weight):
    rows_own = tokens.shape[0]
    columns_dev = gate_weight.shape[1]

    def between(pairs, cross=0):
        return [(s * CORES + c, t * CORES + (c ^ cross)) for s, t in pairs for c in range(CORES)]

    inward = between([(0, 1), (3, 2)])
    outward = between([(1, 0), (2, 3)])
    outward_cross = between([(1, 0), (2, 3)], 1)
    across = between([(1, 2), (2, 1)])
    other_core = [(i, i ^ 1) for i in range(LINE * CORES)]

    def send(x, pairs, name):
        with jax.named_scope(name):
            return lax.ppermute(x, "wide", pairs)

    tiles = half_of(columns_dev) // TILE
    counts = [tiles * p // 116 for p in SHARES]
    counts.append(tiles - sum(counts))
    n = [TILE * t for t in counts]
    chunks = [(sum(n[:i]), n[i]) for i in range(3)]

    mine = gate_weight.T, up_weight.T
    got = send(cut(*mine, 0, sum(n), LARGE), other_core, "swap")
    pack_01, pack_0 = pack(*mine, got, 0, chunks, ((0, 1), (0,)))
    pack_1, pack_2 = pack(*mine, got, 0, chunks, ((1,), (2,)))

    own_01 = send(pack_01, across, "own_01")
    outer_0 = send(pack_0, inward, "outer_0")
    outer_1 = send(after(pack_1, outer_0), inward, "outer_1")
    outer_2 = send(after(pack_2, outer_0), inward, "outer_2")
    far_0 = send(outer_0, across, "far_0")

    here = after(tokens, pack_0)
    blocks = [here] + [lax.ppermute(here, "narrow", [(i, i ^ d) for i in range(LINE)]) for d in (1, 2, 3)]
    x_own, x_give = arrange(blocks)
    x_outer = send(x_give, inward, "x_outer")
    x = x_own, send(x_own, other_core, "x_other"), x_outer, send(x_outer, other_core, "x_outer_other")

    far_1 = send(after(outer_1, own_01), across, "far_1")
    own_2 = send(after(pack_2, far_0), across, "own_2")

    def plan(size, sources):
        step = size if size <= 384 else size // (2 * TILE) * TILE
        cuts = [0, step, size] if step < size else [0, size]
        return [(j, k - j, [(w, g + j, u + j) for w, g, u in sources]) for j, k in zip(cuts[:-1], cuts[1:])]

    def blocks_of(i, rows):
        return plan(n[i], [(k, row, row + n[i]) for k, row in enumerate(rows)])

    second = [2 * n[0]] * 2 + [0] * 2
    far_2 = send(after(outer_2, far_1), across, "far_2")
    weights = [
        [pack_01, own_01, outer_0, far_0],
        [pack_01, own_01, outer_1, far_1],
        [pack_2, own_2, outer_2, far_2],
    ]
    blocks = [blocks_of(0, [0] * 4), blocks_of(1, second), blocks_of(2, [0] * 4)]

    (out,) = outer_hidden(x[2:], weights[0], blocks[0], n[0], True)
    back_0 = send(out, outward, "back_0")
    same, cross = outer_hidden((x[2], x[3]), weights[1], blocks[1], n[1], False)
    back_1 = send(same, outward, "back_1_same"), send(cross, outward_cross, "back_1_cross")
    outs_1 = same
    same, cross = outer_hidden((after(x[2], outs_1), x[3]), weights[2], blocks[2], n[2], False)
    back_2 = send(same, outward, "back_2_same"), send(cross, outward_cross, "back_2_cross")
    own = [(after(x[0], out), x[1]), (after(x[0], outs_1), x[1]), (after(x[0], same), x[1])]

    result = jax.ShapeDtypeStruct((columns_dev, rows_own), jnp.bfloat16)
    result, swap = own_hidden(own[0], weights[0], blocks[0], *chunks[0], result)
    swapped_0 = send(swap, other_core, "swapped_0")
    result, swap = own_hidden(
        own[1], weights[1], blocks[1], *chunks[1], result, swapped=(swapped_0, (chunks[0], None)), back=(back_0, 0)
    )
    swapped_1 = send(swap, other_core, "swapped_1")
    result, swap = own_hidden(
        own[2], weights[2], blocks[2], *chunks[2], result, swapped=(swapped_1, (chunks[1], chunks[0]))
    )
    swapped_2 = send(after(swap, back_2[0], *back_1), other_core, "swapped_2")
    result = put(result, back_1, ([], [(0, False, *chunks[1]), (1, True, *chunks[1])]))
    stores = [(0, True, *chunks[2])], [(1, False, *chunks[2]), (2, True, *chunks[2])]
    return put(result, (swapped_2, *back_2), stores).T


def solution(mesh):
    in_specs = (P("wide", "narrow"), P("wide", "narrow"), P("wide", "narrow"))
    out_specs = P("wide", "narrow")
    local = folded if mesh.shape["wide"] == LINE * CORES else gathered_everywhere
    return jax.shard_map(local, mesh=mesh, in_specs=in_specs, out_specs=out_specs, check_vma=False)
```

```python
import functools

import jax
import jax.numpy as jnp
from jax import lax
from jax.experimental import pallas as pl
from jax.experimental.pallas import tpu as pltpu
from jax.sharding import PartitionSpec as P

CORES = 2
LINE = 4
TILE = 16
SHARES = (44, 48)
TURN = (0, 3, 1, 2)
VMEM = 24 * 1024 * 1024
SMALL = 1024 * 1024
LARGE = 56 * 1024 * 1024


def gated(gate, up):
    return (jax.nn.silu(gate) * up).astype(jnp.bfloat16)


def gathered_everywhere(tokens, gate_weight, up_weight):
    rows = lax.all_gather(tokens, "narrow", axis=1, tiled=True)
    gate_full = lax.all_gather(gate_weight, "wide", axis=0, tiled=True)
    up_full = lax.all_gather(up_weight, "wide", axis=0, tiled=True)
    gate = jnp.dot(rows, gate_full, preferred_element_type=jnp.float32)
    up = jnp.dot(rows, up_full, preferred_element_type=jnp.float32)
    return gated(gate, up)


def line_position():
    index = lax.axis_index("wide")
    return index // CORES, index % CORES


def at_end():
    chip, _ = line_position()
    return (chip == 0) | (chip == LINE - 1)


def half_start(core, columns):
    return pl.multiple_of(core * (columns - half_of(columns)), TILE)


def half_of(columns):
    return -(-columns // (CORES * TILE)) * TILE


def copy_all(copies):
    for copy in copies:
        copy.start()
    for copy in copies:
        copy.wait()


def strips(size):
    strip = -(-size // (4 * TILE)) * TILE
    return [(at, min(strip, size - at)) for at in range(0, size, strip)]


def cut_kernel(start, size, gate_ref, up_ref, out_ref, sems):
    _, core = line_position()
    theirs = half_start(1 - core, gate_ref.shape[0]) + start
    copies = []
    for k, w in enumerate((gate_ref, up_ref)):
        for at, count in strips(size):
            target = out_ref.at[pl.ds(k * size + at, count)]
            copies.append(pltpu.make_async_copy(w.at[pl.ds(theirs + at, count)], target, sems.at[len(copies)]))
    copy_all(copies)


def cut(gate_t, up_t, start, size, room):
    in_hbm = pl.BlockSpec(memory_space=pltpu.HBM)
    return pl.pallas_call(
        functools.partial(cut_kernel, start, size),
        in_specs=[in_hbm, in_hbm],
        out_specs=pl.BlockSpec(memory_space=pltpu.VMEM),
        out_shape=jax.ShapeDtypeStruct((2 * size, gate_t.shape[1]), gate_t.dtype),
        scratch_shapes=[pltpu.SemaphoreType.DMA((8,))],
        compiler_params=pltpu.CompilerParams(vmem_limit_bytes=room),
        cost_estimate=pl.CostEstimate(flops=0, bytes_accessed=4 * gate_t.size, transcendentals=0),
        name="cut",
    )(gate_t, up_t)


def pack_kernel(chunks, got_start, places, gate_ref, up_ref, got_ref, *refs):
    outs, sems = refs[:-1], refs[-1]
    _, core = line_position()
    columns, depth = gate_ref.shape
    got_size = got_ref.shape[0] // 2
    first = half_start(core, columns)

    def fill(me):
        copies = []
        for o, row, i in places:
            start, size = chunks[i]
            for k, w in enumerate((gate_ref, up_ref)):
                target = outs[o].at[pl.ds(row + k * size, size)]
                mine = target.at[:, pl.ds(me * depth, depth)]
                other = target.at[:, pl.ds((1 - me) * depth, depth)]
                sources = (w.at[pl.ds(first + start, size)], mine), (
                    got_ref.at[pl.ds(k * got_size + start - got_start, size)],
                    other,
                )
                for source, target_part in sources:
                    copies.append(pltpu.make_async_copy(source, target_part, sems.at[len(copies)]))
        copy_all(copies)

    for me in range(CORES):
        pl.when(core == me)(functools.partial(fill, me))


def pack(gate_t, up_t, got, got_start, chunks, wanted):
    depth = gate_t.shape[1]
    in_hbm = pl.BlockSpec(memory_space=pltpu.HBM)
    whole = pl.BlockSpec(memory_space=pltpu.VMEM)
    places, out_shape = [], []
    for o, group in enumerate(wanted):
        row = 0
        for i in group:
            places.append((o, row, i))
            row += 2 * chunks[i][1]
        out_shape.append(jax.ShapeDtypeStruct((row, CORES * depth), gate_t.dtype))
    return pl.pallas_call(
        functools.partial(pack_kernel, chunks, got_start, places),
        in_specs=[in_hbm, in_hbm, whole],
        out_specs=[whole] * len(wanted),
        out_shape=out_shape,
        scratch_shapes=[pltpu.SemaphoreType.DMA((4 * len(places),))],
        compiler_params=pltpu.CompilerParams(vmem_limit_bytes=SMALL),
        cost_estimate=pl.CostEstimate(flops=0, bytes_accessed=8 * gate_t.size, transcendentals=0),
        name="pack",
    )(gate_t, up_t, got)


def arrange_kernel(*refs):
    blocks, outs = refs[:LINE], refs[LINE:]
    chip, _ = line_position()
    group = lax.axis_index("narrow")
    features = blocks[0].shape[1]
    for d, block in enumerate(blocks):
        turned = block[...].T
        for out, at in zip(outs, (chip, chip ^ 1)):
            want = at ^ group ^ d
            place = jnp.where(want == TURN[1], 1, jnp.where(want == TURN[2], 2, jnp.where(want == TURN[3], 3, 0)))
            out[pl.ds(pl.multiple_of(place * features, features), features), :] = turned


def arrange(blocks):
    rows, features = blocks[0].shape
    whole = pl.BlockSpec(memory_space=pltpu.VMEM)
    return pl.pallas_call(
        arrange_kernel,
        in_specs=[whole] * LINE,
        out_specs=[whole] * 2,
        out_shape=[jax.ShapeDtypeStruct((LINE * features, rows), blocks[0].dtype)] * 2,
        compiler_params=pltpu.CompilerParams(vmem_limit_bytes=4 * SMALL),
        cost_estimate=pl.CostEstimate(flops=0, bytes_accessed=4 * LINE * blocks[0].size, transcendentals=0),
        name="arrange",
    )(*blocks)


def store(result_ref, parts, sems, at=0):
    _, core = line_position()
    columns = result_ref.shape[0]
    copies = []
    for k, (ref, others, start) in enumerate(parts):
        first = half_start(1 - core if others else core, columns) + start
        target = result_ref.at[pl.ds(first, ref.shape[0])]
        copies.append(pltpu.make_async_copy(ref, target, sems.at[at + k]))
    return copies


def products(blocks, weights, tokens, outs):
    for j, step, sources in blocks:
        sides = [
            jnp.concatenate([weights[source[0]][pl.ds(source[k], step), :] for source in sources], axis=1)
            for k in (1, 2)
        ]
        both_w = jnp.concatenate(sides, axis=0)
        for tokens_ref, out in zip(tokens, outs):
            both = jnp.dot(both_w, tokens_ref[...], preferred_element_type=jnp.float32)
            out[pl.ds(j, step), :] = gated(both[:step], both[step:])


def outer_kernel(blocks, count, *refs):
    tokens, weights, outs = refs[:2], refs[2 : 2 + count], refs[2 + count :]
    rows = tokens[0].shape[1]
    if len(outs) == 1:
        outs = outs[0].at[:, pl.ds(0, rows)], outs[0].at[:, pl.ds(rows, rows)]
    pl.when(jnp.logical_not(at_end()))(functools.partial(products, blocks, weights, tokens, outs))


def outer_hidden(tokens, weights, blocks, size, joint):
    features, rows = tokens[0].shape
    whole = pl.BlockSpec(memory_space=pltpu.VMEM)
    return pl.pallas_call(
        functools.partial(outer_kernel, blocks, len(weights)),
        in_specs=[whole] * (2 + len(weights)),
        out_specs=[whole] * (1 if joint else 2),
        out_shape=[jax.ShapeDtypeStruct((size, rows * (2 if joint else 1)), tokens[0].dtype)] * (1 if joint else 2),
        compiler_params=pltpu.CompilerParams(vmem_limit_bytes=VMEM),
        cost_estimate=pl.CostEstimate(flops=0, bytes_accessed=2 * size * rows, transcendentals=0),
        name="outer_hidden",
    )(*tokens, *weights)


def own_kernel(plan, *refs):
    start, blocks, swap_stores, back_start, count = plan
    tokens, weights, refs = refs[:2], refs[2 : 2 + count], refs[2 + count :]
    result_ref, swap_ref, own_buf, sems = refs[-4:]
    rows = own_buf.shape[1]

    def swap_store(k):
        if swap_stores is None or swap_stores[k] is None:
            return []
        first, number = swap_stores[k]
        return store(result_ref, [(refs[0].at[pl.ds(0, number)], True, first)], sems, 1)

    @pl.when(jnp.logical_not(at_end()))
    def _():
        copies = swap_store(0)
        for copy in copies:
            copy.start()
        products(blocks, weights, tokens, (own_buf, swap_ref))
        copies += store(result_ref, [(own_buf, False, start)], sems)
        copies[-1].start()
        for copy in copies:
            copy.wait()

    @pl.when(at_end())
    def _():
        copies = swap_store(1)
        if back_start is not None:
            back_ref = refs[1]
            number = back_ref.shape[0]
            copies += store(result_ref, [(back_ref.at[:, pl.ds(0, rows)], False, back_start)], sems)
            copies.append(
                pltpu.make_async_copy(back_ref.at[:, pl.ds(rows, rows)], swap_ref.at[pl.ds(0, number)], sems.at[2])
            )
        copy_all(copies)


def own_hidden(tokens, weights, blocks, start, size, result, swapped=None, back=None):
    rows = tokens[0].shape[1]
    whole = pl.BlockSpec(memory_space=pltpu.VMEM)
    in_hbm = pl.BlockSpec(memory_space=pltpu.HBM)
    operands = [*tokens, *weights]
    swap_rows = size
    if swapped is not None:
        operands.append(swapped[0])
    if back is not None:
        operands.append(back[0])
        swap_rows = max(size, back[0].shape[0])
    in_specs = [whole] * len(operands)
    aliases = {}
    if not isinstance(result, jax.ShapeDtypeStruct):
        aliases = {len(operands): 0}
        operands.append(result)
        in_specs.append(in_hbm)
    plan = (start, blocks, swapped and swapped[1], back and back[1], len(weights))
    return pl.pallas_call(
        functools.partial(own_kernel, plan),
        in_specs=in_specs,
        out_specs=[in_hbm, whole],
        out_shape=[
            jax.ShapeDtypeStruct(result.shape, result.dtype),
            jax.ShapeDtypeStruct((swap_rows, rows), result.dtype),
        ],
        scratch_shapes=[pltpu.VMEM((size, rows), result.dtype), pltpu.SemaphoreType.DMA((3,))],
        input_output_aliases=aliases,
        compiler_params=pltpu.CompilerParams(vmem_limit_bytes=VMEM),
        cost_estimate=pl.CostEstimate(flops=0, bytes_accessed=2 * size * rows, transcendentals=0),
        name="own_hidden",
    )(*operands)


def put_kernel(stores, *refs):
    result_ref, sems = refs[-2:]
    for end in (0, 1):

        @pl.when(at_end() == (end == 1))
        def _():
            parts = [
                (refs[k].at[pl.ds(0, count)], others, first) for k, others, first, count in stores[end]
            ]
            copy_all(store(result_ref, parts, sems))


def put(result, arrays, stores):
    in_hbm = pl.BlockSpec(memory_space=pltpu.HBM)
    return pl.pallas_call(
        functools.partial(put_kernel, stores),
        in_specs=[pl.BlockSpec(memory_space=pltpu.VMEM)] * len(arrays) + [in_hbm],
        out_specs=in_hbm,
        out_shape=jax.ShapeDtypeStruct(result.shape, result.dtype),
        scratch_shapes=[pltpu.SemaphoreType.DMA((len(arrays),))],
        input_output_aliases={len(arrays): 0},
        compiler_params=pltpu.CompilerParams(vmem_limit_bytes=SMALL),
        cost_estimate=pl.CostEstimate(flops=0, bytes_accessed=4 * arrays[0].size, transcendentals=0),
        name="put",
    )(*arrays, result)


def after(x, *earlier):
    return lax.optimization_barrier((x, *earlier))[0]


def folded(tokens, gate_weight, up_weight):
    rows_own = tokens.shape[0]
    columns_dev = gate_weight.shape[1]

    def between(pairs, cross=0):
        return [(s * CORES + c, t * CORES + (c ^ cross)) for s, t in pairs for c in range(CORES)]

    inward = between([(0, 1), (3, 2)])
    outward = between([(1, 0), (2, 3)])
    outward_cross = between([(1, 0), (2, 3)], 1)
    across = between([(1, 2), (2, 1)])
    other_core = [(i, i ^ 1) for i in range(LINE * CORES)]

    def send(x, pairs, name):
        with jax.named_scope(name):
            return lax.ppermute(x, "wide", pairs)

    tiles = half_of(columns_dev) // TILE
    counts = [tiles * p // 116 for p in SHARES]
    counts.append(tiles - sum(counts))
    n = [TILE * t for t in counts]
    chunks = [(sum(n[:i]), n[i]) for i in range(3)]

    mine = gate_weight.T, up_weight.T
    got = send(cut(*mine, 0, sum(n), LARGE), other_core, "swap")
    pack_01, pack_0 = pack(*mine, got, 0, chunks, ((0, 1), (0,)))
    pack_1, pack_2 = pack(*mine, got, 0, chunks, ((1,), (2,)))

    own_01 = send(pack_01, across, "own_01")
    outer_0 = send(pack_0, inward, "outer_0")
    outer_1 = send(after(pack_1, outer_0), inward, "outer_1")
    outer_2 = send(after(pack_2, outer_0), inward, "outer_2")
    far_0 = send(outer_0, across, "far_0")

    here = after(tokens, pack_0)
    blocks = [here] + [lax.ppermute(here, "narrow", [(i, i ^ d) for i in range(LINE)]) for d in (1, 2, 3)]
    x_own, x_give = arrange(blocks)
    x_outer = send(x_give, inward, "x_outer")
    x = x_own, send(x_own, other_core, "x_other"), x_outer, send(x_outer, other_core, "x_outer_other")

    far_1 = send(after(outer_1, own_01, x[3]), across, "far_1")
    own_2 = send(after(pack_2, far_0), across, "own_2")

    def plan(size, sources):
        step = size if size <= 384 else size // (2 * TILE) * TILE
        cuts = [0, step, size] if step < size else [0, size]
        return [(j, k - j, [(w, g + j, u + j) for w, g, u in sources]) for j, k in zip(cuts[:-1], cuts[1:])]

    def blocks_of(i, rows):
        return plan(n[i], [(k, row, row + n[i]) for k, row in enumerate(rows)])

    second = [2 * n[0]] * 2 + [0] * 2
    weights = [
        [pack_01, own_01, outer_0, far_0],
        [pack_01, own_01, outer_1, far_1],
    ]
    blocks = [blocks_of(0, [0] * 4), blocks_of(1, second), blocks_of(2, [0] * 4)]

    (out,) = outer_hidden(x[2:], weights[0], blocks[0], n[0], True)
    back_0 = send(out, outward, "back_0")
    result = jax.ShapeDtypeStruct((columns_dev, rows_own), jnp.bfloat16)
    first_own = after(x[0], out), x[1]
    result, swap = own_hidden(first_own, weights[0], blocks[0], *chunks[0], result)
    swapped_0 = send(swap, other_core, "swapped_0")
    (out_1,) = outer_hidden((after(x[2], swap), x[3]), weights[1], blocks[1], n[1], True)
    back_1 = send(out_1, outward, "back_1")
    far_2 = send(after(outer_2, out_1), across, "far_2")
    weights.append([pack_2, own_2, outer_2, far_2])
    same, cross = outer_hidden((after(x[2], out_1), x[3]), weights[2], blocks[2], n[2], False)
    back_2 = send(same, outward, "back_2_same"), send(cross, outward_cross, "back_2_cross")
    own = [None, (after(x[0], out_1, own_2), x[1]), (after(x[0], same), x[1])]

    result, swap = own_hidden(
        own[1], weights[1], blocks[1], *chunks[1], result, swapped=(swapped_0, (chunks[0], None)), back=(back_0, 0)
    )
    swapped_1 = send(swap, other_core, "swapped_1")
    result, swap = own_hidden(
        own[2], weights[2], blocks[2], *chunks[2], result, swapped=(swapped_1, (chunks[1], chunks[0])), back=(back_1, chunks[1][0])
    )
    swapped_2 = send(after(swap, *back_2), other_core, "swapped_2")
    stores = [(0, True, *chunks[2])], [(0, True, *chunks[1]), (1, False, *chunks[2]), (2, True, *chunks[2])]
    return put(result, (swapped_2, *back_2), stores).T


def solution(mesh):
    in_specs = (P("wide", "narrow"), P("wide", "narrow"), P("wide", "narrow"))
    out_specs = P("wide", "narrow")
    local = folded if mesh.shape["wide"] == LINE * CORES else gathered_everywhere
    return jax.shard_map(local, mesh=mesh, in_specs=in_specs, out_specs=out_specs, check_vma=False)
```

```python
import functools

import jax
import jax.numpy as jnp
from jax import lax
from jax.experimental import pallas as pl
from jax.experimental.pallas import tpu as pltpu
from jax.sharding import PartitionSpec as P

CORES = 2
LINE = 4
TILE = 16
SHARES = (44, 48)
TURN = (0, 3, 1, 2)
VMEM = 24 * 1024 * 1024
SMALL = 1024 * 1024
LARGE = 56 * 1024 * 1024


def gated(gate, up):
    return (jax.nn.silu(gate) * up).astype(jnp.bfloat16)


def gathered_everywhere(tokens, gate_weight, up_weight):
    rows = lax.all_gather(tokens, "narrow", axis=1, tiled=True)
    gate_full = lax.all_gather(gate_weight, "wide", axis=0, tiled=True)
    up_full = lax.all_gather(up_weight, "wide", axis=0, tiled=True)
    gate = jnp.dot(rows, gate_full, preferred_element_type=jnp.float32)
    up = jnp.dot(rows, up_full, preferred_element_type=jnp.float32)
    return gated(gate, up)


def line_position():
    index = lax.axis_index("wide")
    return index // CORES, index % CORES


def at_end():
    chip, _ = line_position()
    return (chip == 0) | (chip == LINE - 1)


def half_start(core, columns):
    return pl.multiple_of(core * (columns - half_of(columns)), TILE)


def half_of(columns):
    return -(-columns // (CORES * TILE)) * TILE


def copy_all(copies):
    for copy in copies:
        copy.start()
    for copy in copies:
        copy.wait()


def strips(size):
    strip = -(-size // (4 * TILE)) * TILE
    return [(at, min(strip, size - at)) for at in range(0, size, strip)]


def cut_kernel(start, size, gate_ref, up_ref, out_ref, sems):
    _, core = line_position()
    theirs = half_start(1 - core, gate_ref.shape[0]) + start
    copies = []
    for k, w in enumerate((gate_ref, up_ref)):
        for at, count in strips(size):
            target = out_ref.at[pl.ds(k * size + at, count)]
            copies.append(pltpu.make_async_copy(w.at[pl.ds(theirs + at, count)], target, sems.at[len(copies)]))
    copy_all(copies)


def cut(gate_t, up_t, start, size, room):
    in_hbm = pl.BlockSpec(memory_space=pltpu.HBM)
    return pl.pallas_call(
        functools.partial(cut_kernel, start, size),
        in_specs=[in_hbm, in_hbm],
        out_specs=pl.BlockSpec(memory_space=pltpu.VMEM),
        out_shape=jax.ShapeDtypeStruct((2 * size, gate_t.shape[1]), gate_t.dtype),
        scratch_shapes=[pltpu.SemaphoreType.DMA((8,))],
        compiler_params=pltpu.CompilerParams(vmem_limit_bytes=room),
        cost_estimate=pl.CostEstimate(flops=0, bytes_accessed=4 * gate_t.size, transcendentals=0),
        name="cut",
    )(gate_t, up_t)


def pack_kernel(chunks, got_start, places, gate_ref, up_ref, got_ref, *refs):
    outs, sems = refs[:-1], refs[-1]
    _, core = line_position()
    columns, depth = gate_ref.shape
    got_size = got_ref.shape[0] // 2
    first = half_start(core, columns)

    def fill(me):
        copies = []
        for o, row, i in places:
            start, size = chunks[i]
            for k, w in enumerate((gate_ref, up_ref)):
                target = outs[o].at[pl.ds(row + k * size, size)]
                mine = target.at[:, pl.ds(me * depth, depth)]
                other = target.at[:, pl.ds((1 - me) * depth, depth)]
                sources = (w.at[pl.ds(first + start, size)], mine), (
                    got_ref.at[pl.ds(k * got_size + start - got_start, size)],
                    other,
                )
                for source, target_part in sources:
                    copies.append(pltpu.make_async_copy(source, target_part, sems.at[len(copies)]))
        copy_all(copies)

    for me in range(CORES):
        pl.when(core == me)(functools.partial(fill, me))


def pack(gate_t, up_t, got, got_start, chunks, wanted):
    depth = gate_t.shape[1]
    in_hbm = pl.BlockSpec(memory_space=pltpu.HBM)
    whole = pl.BlockSpec(memory_space=pltpu.VMEM)
    places, out_shape = [], []
    for o, group in enumerate(wanted):
        row = 0
        for i in group:
            places.append((o, row, i))
            row += 2 * chunks[i][1]
        out_shape.append(jax.ShapeDtypeStruct((row, CORES * depth), gate_t.dtype))
    return pl.pallas_call(
        functools.partial(pack_kernel, chunks, got_start, places),
        in_specs=[in_hbm, in_hbm, whole],
        out_specs=[whole] * len(wanted),
        out_shape=out_shape,
        scratch_shapes=[pltpu.SemaphoreType.DMA((4 * len(places),))],
        compiler_params=pltpu.CompilerParams(vmem_limit_bytes=SMALL),
        cost_estimate=pl.CostEstimate(flops=0, bytes_accessed=8 * gate_t.size, transcendentals=0),
        name="pack",
    )(gate_t, up_t, got)


def arrange_kernel(*refs):
    blocks, outs = refs[:LINE], refs[LINE:]
    chip, _ = line_position()
    group = lax.axis_index("narrow")
    features = blocks[0].shape[1]
    for d, block in enumerate(blocks):
        turned = block[...].T
        for out, at in zip(outs, (chip, chip ^ 1)):
            want = at ^ group ^ d
            place = jnp.where(want == TURN[1], 1, jnp.where(want == TURN[2], 2, jnp.where(want == TURN[3], 3, 0)))
            out[pl.ds(pl.multiple_of(place * features, features), features), :] = turned


def arrange(blocks):
    rows, features = blocks[0].shape
    whole = pl.BlockSpec(memory_space=pltpu.VMEM)
    return pl.pallas_call(
        arrange_kernel,
        in_specs=[whole] * LINE,
        out_specs=[whole] * 2,
        out_shape=[jax.ShapeDtypeStruct((LINE * features, rows), blocks[0].dtype)] * 2,
        compiler_params=pltpu.CompilerParams(vmem_limit_bytes=4 * SMALL),
        cost_estimate=pl.CostEstimate(flops=0, bytes_accessed=4 * LINE * blocks[0].size, transcendentals=0),
        name="arrange",
    )(*blocks)


def store(result_ref, parts, sems, at=0):
    _, core = line_position()
    columns = result_ref.shape[0]
    copies = []
    for k, (ref, others, start) in enumerate(parts):
        first = half_start(1 - core if others else core, columns) + start
        target = result_ref.at[pl.ds(first, ref.shape[0])]
        copies.append(pltpu.make_async_copy(ref, target, sems.at[at + k]))
    return copies


def products(blocks, weights, tokens, outs):
    for j, step, sources in blocks:
        sides = [
            jnp.concatenate([weights[source[0]][pl.ds(source[k], step), :] for source in sources], axis=1)
            for k in (1, 2)
        ]
        both_w = jnp.concatenate(sides, axis=0)
        for tokens_ref, out in zip(tokens, outs):
            both = jnp.dot(both_w, tokens_ref[...], preferred_element_type=jnp.float32)
            out[pl.ds(j, step), :] = gated(both[:step], both[step:])


def outer_kernel(blocks, count, *refs):
    tokens, weights, outs = refs[:2], refs[2 : 2 + count], refs[2 + count :]
    rows = tokens[0].shape[1]
    if len(outs) == 1:
        outs = outs[0].at[:, pl.ds(0, rows)], outs[0].at[:, pl.ds(rows, rows)]
    pl.when(jnp.logical_not(at_end()))(functools.partial(products, blocks, weights, tokens, outs))


def outer_hidden(tokens, weights, blocks, size, joint):
    features, rows = tokens[0].shape
    whole = pl.BlockSpec(memory_space=pltpu.VMEM)
    return pl.pallas_call(
        functools.partial(outer_kernel, blocks, len(weights)),
        in_specs=[whole] * (2 + len(weights)),
        out_specs=[whole] * (1 if joint else 2),
        out_shape=[jax.ShapeDtypeStruct((size, rows * (2 if joint else 1)), tokens[0].dtype)] * (1 if joint else 2),
        compiler_params=pltpu.CompilerParams(vmem_limit_bytes=VMEM),
        cost_estimate=pl.CostEstimate(flops=0, bytes_accessed=2 * size * rows, transcendentals=0),
        name="outer_hidden",
    )(*tokens, *weights)


def own_kernel(plan, *refs):
    start, blocks, swap_stores, back_start, count = plan
    tokens, weights, refs = refs[:2], refs[2 : 2 + count], refs[2 + count :]
    result_ref, swap_ref, own_buf, sems = refs[-4:]
    rows = own_buf.shape[1]

    def swap_store(k):
        if swap_stores is None or swap_stores[k] is None:
            return []
        first, number = swap_stores[k]
        return store(result_ref, [(refs[0].at[pl.ds(0, number)], True, first)], sems, 1)

    @pl.when(jnp.logical_not(at_end()))
    def _():
        copies = swap_store(0)
        for copy in copies:
            copy.start()
        products(blocks, weights, tokens, (own_buf, swap_ref))
        copies += store(result_ref, [(own_buf, False, start)], sems)
        copies[-1].start()
        for copy in copies:
            copy.wait()

    @pl.when(at_end())
    def _():
        copies = swap_store(1)
        if back_start is not None:
            back_ref = refs[1]
            number = back_ref.shape[0]
            copies += store(result_ref, [(back_ref.at[:, pl.ds(0, rows)], False, back_start)], sems)
            copies.append(
                pltpu.make_async_copy(back_ref.at[:, pl.ds(rows, rows)], swap_ref.at[pl.ds(0, number)], sems.at[2])
            )
        copy_all(copies)


def own_hidden(tokens, weights, blocks, start, size, result, swapped=None, back=None):
    rows = tokens[0].shape[1]
    whole = pl.BlockSpec(memory_space=pltpu.VMEM)
    in_hbm = pl.BlockSpec(memory_space=pltpu.HBM)
    operands = [*tokens, *weights]
    swap_rows = size
    if swapped is not None:
        operands.append(swapped[0])
    if back is not None:
        operands.append(back[0])
        swap_rows = max(size, back[0].shape[0])
    in_specs = [whole] * len(operands)
    aliases = {}
    if not isinstance(result, jax.ShapeDtypeStruct):
        aliases = {len(operands): 0}
        operands.append(result)
        in_specs.append(in_hbm)
    plan = (start, blocks, swapped and swapped[1], back and back[1], len(weights))
    return pl.pallas_call(
        functools.partial(own_kernel, plan),
        in_specs=in_specs,
        out_specs=[in_hbm, whole],
        out_shape=[
            jax.ShapeDtypeStruct(result.shape, result.dtype),
            jax.ShapeDtypeStruct((swap_rows, rows), result.dtype),
        ],
        scratch_shapes=[pltpu.VMEM((size, rows), result.dtype), pltpu.SemaphoreType.DMA((3,))],
        input_output_aliases=aliases,
        compiler_params=pltpu.CompilerParams(vmem_limit_bytes=VMEM),
        cost_estimate=pl.CostEstimate(flops=0, bytes_accessed=2 * size * rows, transcendentals=0),
        name="own_hidden",
    )(*operands)


def put_kernel(stores, *refs):
    result_ref, sems = refs[-2:]
    for end in (0, 1):

        @pl.when(at_end() == (end == 1))
        def _():
            parts = [
                (refs[k].at[pl.ds(0, count)], others, first) for k, others, first, count in stores[end]
            ]
            copy_all(store(result_ref, parts, sems))


def put(result, arrays, stores):
    in_hbm = pl.BlockSpec(memory_space=pltpu.HBM)
    return pl.pallas_call(
        functools.partial(put_kernel, stores),
        in_specs=[pl.BlockSpec(memory_space=pltpu.VMEM)] * len(arrays) + [in_hbm],
        out_specs=in_hbm,
        out_shape=jax.ShapeDtypeStruct(result.shape, result.dtype),
        scratch_shapes=[pltpu.SemaphoreType.DMA((len(arrays),))],
        input_output_aliases={len(arrays): 0},
        compiler_params=pltpu.CompilerParams(vmem_limit_bytes=SMALL),
        cost_estimate=pl.CostEstimate(flops=0, bytes_accessed=4 * arrays[0].size, transcendentals=0),
        name="put",
    )(*arrays, result)


def after(x, *earlier):
    return lax.optimization_barrier((x, *earlier))[0]


def folded(tokens, gate_weight, up_weight):
    rows_own = tokens.shape[0]
    columns_dev = gate_weight.shape[1]

    def between(pairs, cross=0):
        return [(s * CORES + c, t * CORES + (c ^ cross)) for s, t in pairs for c in range(CORES)]

    inward = between([(0, 1), (3, 2)])
    outward = between([(1, 0), (2, 3)])
    outward_cross = between([(1, 0), (2, 3)], 1)
    across = between([(1, 2), (2, 1)])
    other_core = [(i, i ^ 1) for i in range(LINE * CORES)]

    def send(x, pairs, name):
        with jax.named_scope(name):
            return lax.ppermute(x, "wide", pairs)

    tiles = half_of(columns_dev) // TILE
    counts = [tiles * p // 116 for p in SHARES]
    counts.append(tiles - sum(counts))
    n = [TILE * t for t in counts]
    chunks = [(sum(n[:i]), n[i]) for i in range(3)]

    mine = gate_weight.T, up_weight.T
    first = n[0] + n[1]
    got = send(cut(*mine, 0, first, LARGE), other_core, "swap")
    pack_01, pack_0 = pack(*mine, got, 0, chunks, ((0, 1), (0,)))
    (pack_1,) = pack(*mine, got, 0, chunks, ((1,),))
    rest = [after(w, pack_0) for w in mine]
    got_rest = send(cut(*rest, first, n[2], SMALL), other_core, "swap_rest")
    (pack_2,) = pack(*mine, got_rest, first, chunks, ((2,),))

    own_01 = send(pack_01, across, "own_01")
    outer_0 = send(pack_0, inward, "outer_0")
    outer_1 = send(after(pack_1, outer_0), inward, "outer_1")
    outer_2 = send(after(pack_2, outer_0), inward, "outer_2")
    far_0 = send(outer_0, across, "far_0")

    here = after(tokens, pack_0)
    blocks = [here] + [lax.ppermute(here, "narrow", [(i, i ^ d) for i in range(LINE)]) for d in (1, 2, 3)]
    x_own, x_give = arrange(blocks)
    x_outer = send(x_give, inward, "x_outer")
    x = x_own, send(x_own, other_core, "x_other"), x_outer, send(x_outer, other_core, "x_outer_other")

    far_1 = send(after(outer_1, own_01, x[3]), across, "far_1")
    own_2 = send(after(pack_2, far_0), across, "own_2")

    def plan(size, sources):
        step = size if size <= 384 else size // (2 * TILE) * TILE
        cuts = [0, step, size] if step < size else [0, size]
        return [(j, k - j, [(w, g + j, u + j) for w, g, u in sources]) for j, k in zip(cuts[:-1], cuts[1:])]

    def blocks_of(i, rows):
        return plan(n[i], [(k, row, row + n[i]) for k, row in enumerate(rows)])

    second = [2 * n[0]] * 2 + [0] * 2
    weights = [
        [pack_01, own_01, outer_0, far_0],
        [pack_01, own_01, outer_1, far_1],
    ]
    blocks = [blocks_of(0, [0] * 4), blocks_of(1, second), blocks_of(2, [0] * 4)]

    (out,) = outer_hidden(x[2:], weights[0], blocks[0], n[0], True)
    back_0 = send(out, outward, "back_0")
    result = jax.ShapeDtypeStruct((columns_dev, rows_own), jnp.bfloat16)
    first_own = after(x[0], out), x[1]
    result, swap = own_hidden(first_own, weights[0], blocks[0], *chunks[0], result)
    swapped_0 = send(swap, other_core, "swapped_0")
    (out_1,) = outer_hidden((after(x[2], swap), x[3]), weights[1], blocks[1], n[1], True)
    back_1 = send(out_1, outward, "back_1")
    far_2 = send(after(outer_2, out_1), across, "far_2")
    weights.append([pack_2, own_2, outer_2, far_2])
    same, cross = outer_hidden((after(x[2], out_1), x[3]), weights[2], blocks[2], n[2], False)
    back_2 = send(same, outward, "back_2_same"), send(cross, outward_cross, "back_2_cross")
    own = [None, (after(x[0], out_1, own_2), x[1]), (after(x[0], same), x[1])]

    result, swap = own_hidden(
        own[1], weights[1], blocks[1], *chunks[1], result, swapped=(swapped_0, (chunks[0], None)), back=(back_0, 0)
    )
    swapped_1 = send(swap, other_core, "swapped_1")
    result, swap = own_hidden(
        own[2], weights[2], blocks[2], *chunks[2], result, swapped=(swapped_1, (chunks[1], chunks[0])), back=(back_1, chunks[1][0])
    )
    swapped_2 = send(after(swap, *back_2), other_core, "swapped_2")
    stores = [(0, True, *chunks[2])], [(0, True, *chunks[1]), (1, False, *chunks[2]), (2, True, *chunks[2])]
    return put(result, (swapped_2, *back_2), stores).T


def solution(mesh):
    in_specs = (P("wide", "narrow"), P("wide", "narrow"), P("wide", "narrow"))
    out_specs = P("wide", "narrow")
    local = folded if mesh.shape["wide"] == LINE * CORES else gathered_everywhere
    return jax.shard_map(local, mesh=mesh, in_specs=in_specs, out_specs=out_specs, check_vma=False)
```
